32 devices in a mesh: groups: 2 (over y), slide: 4 (over x, core), band: 4 (over z).
Axes of the slice: x: 2, y: 2, z: 4, core: 2. Of those that a mesh axis runs over, the one named last changes fastest.
Arguments:
- features: bfloat16 [8, 4, 256, 192], P(('groups', 'slide'), 'band'), parts along dimension 0, may hold values from -6 to 6
- tissue: int32 [8, 4, 2], P(('groups', 'slide'), 'band'), parts along dimension 0, may hold values 0 or 1
- cotangent: bfloat16 [8, 4, 256, 192], P(('groups', 'slide'), None, 'band'), parts along dimension 0, may hold values from -6 to 6
- x_proj: float32 [4, 192, 38], replicated, may hold values from -0.4375 to 0.4375
- dt_proj: float32 [4, 6, 192], replicated, may hold values from -2.5 to 2.5
- dt_bias: float32 [4, 192], replicated, may hold values from -6 to -2
- a_log: float32 [4, 16, 192], replicated, may hold values from 0 to 2.77
- d_skip: float32 [4, 192], replicated, may hold values from 0.5 to 1.5
Outputs:
- mixed: bfloat16 [8, 4, 256, 192], P(('groups', 'slide'), None, 'band'), parts along dimension 0
- grad_features: bfloat16 [8, 4, 256, 192], P(('groups', 'slide'), 'band'), parts along dimension 0
- grad_x_proj: float32 [8, 192, 38], P('groups'), parts along dimension 0
- grad_dt_proj: float32 [8, 6, 192], P('groups'), parts along dimension 0
- grad_dt_bias: float32 [8, 192], P('groups'), parts along dimension 0
- grad_a_log: float32 [8, 16, 192], P('groups'), parts along dimension 0
- grad_d_skip: float32 [8, 192], P('groups'), parts along dimension 0
The draws below stay inside these ranges and needn't reach their ends.
There are 2 independent parts, one for each index of `groups`. The reference program is written for one: setup_inputs(seed, part) draws one part's arguments, and reference() takes and returns one part's arrays. A program takes and returns all parts, laid end to end along the dimension named above; an argument that names none is the same for every part. Nothing has to cross between parts.
Inputs may be any that keep to these rules, and one draw needn't show every extreme that they name: 1 marks a tile of 128 tokens of one row that holds tissue, 0 one without.
All inputs are finite; a program needn't handle non-finite values. No bound on the sum of `tissue` on one device may be relied on, other than what follows from the above.
Results may differ from the reference program's by a relative error of at most 0.015.
Values may be sent and summed in bfloat16 or wider, within the bound.
A program may use at most 192 MiB of HBM per device.

```python
import jax
import jax.numpy as jnp
from jax import lax

C = 192
N = 16
R = 6
K = 4
TILE = 128
W = 256
SLIDES = 4
H = 4
WT = 2


def plant(values, stream_key, least, top_value):
    spot = [jax.random.randint(jax.random.fold_in(stream_key, axis), (), 0, length) for axis, length in enumerate(values.shape)]
    widest = values.shape.index(max(values.shape))
    beside = spot[:widest] + [(spot[widest] + 1) % values.shape[widest]] + spot[widest + 1:]
    return values.at[tuple(spot)].set(least).at[tuple(beside)].set(top_value)


def levels(key, extent, split, least, top_value):
    level, own = 1.0, jax.random.fold_in(key, 6)
    for axis_at, blocks in split:
        heights = jnp.exp(jax.random.uniform(jax.random.fold_in(own, axis_at), (blocks,), jnp.float32, least / len(split), top_value / len(split)))
        level = level * jnp.repeat(heights, extent[axis_at] // blocks).reshape([-1 if axis == axis_at else 1 for axis in range(len(extent))])
    return level


def scatter_about(rng, dims, spread, bound, pieces=(), held_as=jnp.bfloat16):
    array = jax.random.normal(rng, dims, jnp.float32) * spread
    if len(pieces) > 0:
        array = levels(rng, dims, pieces, -0.22, 0.18) * array
    return jnp.clip(array, min=-bound, max=bound).astype(held_as)


def setup_inputs(seed: int = 0, part: int = 0) -> dict:
    streams_of = jax.random.split(jax.random.key(seed), 9)
    part_splits = jax.random.split(jax.random.fold_in(streams_of[8], part), 9)
    return {
        "features": scatter_about(part_splits[0], (SLIDES, H, W, C), 1.0, 6.0, ((0, 4), (1, 4))),
        "tissue": plant((jax.random.randint(part_splits[1], (SLIDES, H, WT), 0, 4) < 3).astype(jnp.int32), jax.random.fold_in(part_splits[1], 1), 0, 1),
        "cotangent": scatter_about(part_splits[2], (SLIDES, H, W, C), 1.0, 6.0, ((0, 4), (2, 4))),
        "x_proj": scatter_about(streams_of[3], (K, C, R + 2 * N), C ** -0.5, 0.4375, (), jnp.float32),
        "dt_proj": scatter_about(streams_of[4], (K, R, C), R ** -0.5, 2.5, (), jnp.float32),
        "dt_bias": jnp.clip(jax.random.uniform(streams_of[5], (K, C), jnp.float32, -6.0, -2.0), -6.0, -2.0),
        "a_log": jnp.clip(jax.random.uniform(streams_of[6], (K, N, C), jnp.float32, 0.0, 2.77), 0.0, 2.77),
        "d_skip": jnp.clip(1.0 + 0.1 * jax.random.normal(streams_of[7], (K, C), jnp.float32), 0.5, 1.5),
    }


def direction_scan(inputs, keep_mask, x_weight, dt_weight, dt_offset, log_rate, skip_gain, reverse):
    masked = inputs * keep_mask[:, :, None]
    projected = jnp.einsum('lbc,cr->lbr', masked, x_weight, precision=lax.Precision.HIGHEST)
    rank_size = dt_weight.shape[0]
    state_size = log_rate.shape[0]
    low_rank = projected[:, :, :rank_size]
    b_coef = projected[:, :, rank_size:rank_size + state_size]
    c_coef = projected[:, :, rank_size + state_size:]
    step_size = jax.nn.softplus(jnp.einsum('lbr,rc->lbc', low_rank, dt_weight, precision=lax.Precision.HIGHEST) + dt_offset) * keep_mask[:, :, None]
    decay_rate = -jnp.exp(log_rate)

    def advance(state_now, item):
        step_now, inputs_now, b_now, c_now = item
        state_now = jnp.exp(step_now[:, None, :] * decay_rate) * state_now + (step_now * inputs_now)[:, None, :] * b_now[:, :, None]
        return (state_now, lax.optimization_barrier(jnp.sum(c_now[:, :, None] * state_now, axis=1)))
    start = jnp.zeros((inputs.shape[1], state_size, inputs.shape[2]), jnp.float32)
    _, outputs = lax.scan(advance, start, (step_size, masked, b_coef, c_coef), reverse=reverse)
    return outputs + skip_gain * masked

def section(field, keep_mask, section_params, scan_axis):
    sequence = jnp.moveaxis(field, scan_axis, 0)
    seq_shape = sequence.shape
    sequence = sequence.reshape(seq_shape[0], -1, seq_shape[-1])
    mask_seq = jnp.moveaxis(keep_mask, scan_axis, 0).reshape(seq_shape[0], -1)
    x_weight, dt_weight, dt_offset, log_rate, skip_gain = section_params
    summed = direction_scan(sequence, mask_seq, x_weight[0], dt_weight[0], dt_offset[0], log_rate[0], skip_gain[0], False)
    summed = summed + direction_scan(sequence, mask_seq, x_weight[1], dt_weight[1], dt_offset[1], log_rate[1], skip_gain[1], True)
    return jnp.moveaxis(summed.reshape(seq_shape), 0, scan_axis)

def reference(features, tissue, cotangent, x_proj, dt_proj, dt_bias, a_log, d_skip):
    keep_mask = jnp.repeat(tissue, TILE, axis=2).astype(jnp.float32)
    weights = (x_proj, dt_proj, dt_bias, a_log, d_skip)
    horiz_params = tuple((weight[:2] for weight in weights))
    vert_params = tuple((weight[2:] for weight in weights))

    def horizontal(feature_in, section_params):
        return section(feature_in.astype(jnp.float32), keep_mask, section_params, 2)

    def vertical(carried_in, section_params):
        return section(carried_in.astype(jnp.float32), keep_mask, section_params, 1)
    rows_out, pull_rows = jax.vjp(horizontal, features, horiz_params)
    carried = rows_out.astype(jnp.bfloat16)
    cols_out, pull_cols = jax.vjp(vertical, carried, vert_params)
    grad_carried, grad_vert = pull_cols(cotangent.astype(jnp.float32))
    grad_features, grad_horiz = pull_rows(grad_carried.astype(jnp.float32))
    joined = tuple((jnp.concatenate([first_part, second_part], axis=0) for first_part, second_part in zip(grad_horiz, grad_vert)))
    return (cols_out.astype(jnp.bfloat16), grad_features, joined[0], joined[1], joined[2], joined[3], joined[4])
```

```python
import functools
import math

import jax
import jax.numpy as jnp
from jax import lax
from jax.experimental import pallas as pl
from jax.experimental.pallas import tpu as pltpu
from jax.sharding import PartitionSpec as P

BF = jnp.bfloat16
F32 = jnp.float32
SUB = 8
LANES = 128
LOG2E = math.log2(math.e)


def up(value, unit):
    return -(-value // unit) * unit


def mm(a, b, dims=((1,), (0,))):
    return lax.dot_general(a.astype(BF), b.astype(BF), (dims, ((), ())), preferred_element_type=F32)


def split(a):
    high = a.astype(BF)
    return high, (a - high.astype(F32)).astype(BF)


def mm_exact_left(a, b):
    high, low = split(b)
    return mm(a, high) + mm(a, low)


def mm_exact_right(a, b):
    high, low = split(a)
    return mm(high, b) + mm(low, b)


def mm_three(a, b):
    high, low = split(a)
    return mm_exact_left(high, b) + mm(low, b)


class Sizes:
    def __init__(self, channels, rank, states, steps, seqs):
        self.C, self.R, self.N = channels, rank, states
        self.CP = up(channels + 1, LANES)
        self.L, self.M = steps, seqs
        self.T = steps * seqs
        self.XR = up(rank + 2 * states, SUB)
        self.DR = up(rank, SUB)
        self.rows = self.XR + self.DR + SUB + up(states, SUB)

    def scratch(self):
        t, cp, n = self.T, self.CP, self.N
        wide, narrow = (t, n * cp), (t, n * LANES)
        shapes = dict(
            a=wide, h=wide, bb=narrow, cb=narrow, qb=narrow, qc=narrow,
            u=(t, cp), m=(t, cp), gy=(t, cp), dt=(t, cp), du=(t, cp), z=(t, cp), p=(t, LANES),
            y=(t, cp), s=(t, cp), dd=(t, cp), dv=(t, cp),
            xw=(2, cp, LANES), dw=(2, LANES, cp), bias=(2, SUB, cp), skip=(2, SUB, cp),
            rate=(2 * n, cp), drate=(SUB, n * cp), edge=(SUB, n * cp),
        )
        return shapes


def load_weights(sz, S, x_ref, d_ref, b_ref, l_ref, k_ref):
    for name in ("xw", "dw", "bias", "skip", "rate"):
        S[name][...] = jnp.zeros_like(S[name])
    for k in range(2):
        S["xw"][k, : sz.C, : sz.R + 2 * sz.N] = x_ref[k]
        S["dw"][k, : sz.R, : sz.C] = d_ref[k]
        S["bias"][k, :, : sz.C] = jnp.broadcast_to(b_ref[k : k + 1, :], (SUB, sz.C))
        S["skip"][k, :, : sz.C] = jnp.broadcast_to(k_ref[k : k + 1, :], (SUB, sz.C))
        S["rate"][k * sz.N : (k + 1) * sz.N, : sz.C] = -jnp.exp(l_ref[k])


def prepare(sz, S, k):
    u = S["u"][...]
    p = mm_exact_left(u, S["xw"][k])
    z = mm_three(p, S["dw"][k]) + S["bias"][k, 0:1, :]
    dt = (jnp.maximum(z, 0.0) + jnp.log1p(jnp.exp(-jnp.abs(z)))) * S["m"][...]
    S["p"][...] = p
    S["z"][...] = z
    S["dt"][...] = dt
    S["du"][...] = dt * u
    row = lax.broadcasted_iota(jnp.int32, (LANES, LANES), 0)
    for n in range(sz.N):
        cut = slice(n * LANES, (n + 1) * LANES)
        S["bb"][:, cut] = mm_exact_right(p, (row == sz.R + n).astype(F32))
        S["cb"][:, cut] = mm_exact_right(p, (row == sz.R + sz.N + n).astype(F32))


def wide(sz, n):
    return slice(n * sz.CP, (n + 1) * sz.CP)


def both(sz, value):
    return jnp.concatenate([value] * (sz.CP // LANES), axis=1)


def fold(sz, value):
    total = value[:, :LANES]
    for at in range(LANES, sz.CP, LANES):
        total = total + value[:, at : at + LANES]
    return total


def rows_of(sz, step, group, backwards):
    place = sz.L - 1 - step if backwards else step
    return pl.ds(pl.multiple_of(place * sz.M + group * SUB, SUB), SUB)


def rate_row(sz, S, k, n):
    return jnp.broadcast_to(S["rate"][k * sz.N + n : k * sz.N + n + 1, :], (SUB, sz.CP))


def b_of(sz, S, name, at, n):
    return both(sz, S[name][at, n * LANES : (n + 1) * LANES])


def shift(sz, value, backwards):
    row = lax.broadcasted_iota(jnp.int32, value.shape, 0)
    if backwards:
        return jnp.where(row == SUB - 1, 0.0, pltpu.roll(value, SUB - 1, 0))
    return jnp.where(row == 0, 0.0, pltpu.roll(value, 1, 0))


def join_chunks(sz, S, k, ends, backwards):
    total = jnp.zeros((SUB, sz.CP), F32)
    for step in range(sz.L):
        total = total + S["dt"][step * SUB : (step + 1) * SUB, :]
    for n in range(sz.N):
        decay = jnp.exp(total * rate_row(sz, S, k, n))
        start = jnp.zeros((SUB, sz.CP), F32)
        for _ in range(SUB - 1):
            start = shift(sz, decay * start + ends[n], backwards)
        S["edge"][:, wide(sz, n)] = start


def zeros(sz):
    return tuple(jnp.zeros((SUB, sz.CP), F32) for _ in range(sz.N))


def edges(sz, S):
    return tuple(S["edge"][:, wide(sz, n)] for n in range(sz.N))


def local_states(sz, S, k):
    rev = k == 1

    def body(i, h):
        at = rows_of(sz, i, 0, rev)
        dt, du = S["dt"][at, :], S["du"][at, :]
        out = []
        for n in range(sz.N):
            a = jnp.exp2(dt * (LOG2E * rate_row(sz, S, k, n)))
            S["a"][at, wide(sz, n)] = a
            out.append(a * h[n] + du * b_of(sz, S, "bb", at, n))
        return tuple(out)

    join_chunks(sz, S, k, lax.fori_loop(0, sz.L, body, zeros(sz)), rev)


def run_states(sz, S, k, group, start, chunked, want_y, want_grad):
    rev = k == 1

    def body(i, h):
        at = rows_of(sz, i, group, rev)
        dt, du = S["dt"][at, :], S["du"][at, :]
        gy = S["gy"][at, :] if want_grad else None
        y = None
        out = []
        for n in range(sz.N):
            if chunked:
                a = S["a"][at, wide(sz, n)]
            else:
                a = jnp.exp2(dt * (LOG2E * rate_row(sz, S, k, n)))
                S["a"][at, wide(sz, n)] = a
            new = a * h[n] + du * b_of(sz, S, "bb", at, n)
            if want_grad:
                S["h"][at, wide(sz, n)] = h[n]
                S["qc"][at, n * LANES : (n + 1) * LANES] = fold(sz, gy * new)
            if want_y:
                term = new * b_of(sz, S, "cb", at, n)
                y = term if y is None else y + term
            out.append(new)
        if want_y:
            S["y"][at, :] = S["y"][at, :] + y + S["skip"][k] * S["u"][at, :]
        return tuple(out)

    lax.fori_loop(0, sz.L, body, start)


def local_adjoints(sz, S, k):
    rev = k == 0

    def body(i, e):
        at = rows_of(sz, i, 0, rev)
        gy = S["gy"][at, :]
        return tuple(
            S["a"][at, wide(sz, n)] * (b_of(sz, S, "cb", at, n) * gy + e[n]) for n in range(sz.N)
        )

    join_chunks(sz, S, k, lax.fori_loop(0, sz.L, body, zeros(sz)), rev)


def run_adjoints(sz, S, k, group, start):
    rev = k == 0

    def body(i, e):
        at = rows_of(sz, i, group, rev)
        gy, dt, du = S["gy"][at, :], S["dt"][at, :], S["du"][at, :]
        s = dd = None
        out = []
        for n in range(sz.N):
            g = b_of(sz, S, "cb", at, n) * gy + e[n]
            w = S["a"][at, wide(sz, n)] * g
            S["qb"][at, n * LANES : (n + 1) * LANES] = fold(sz, g * du)
            sb = g * b_of(sz, S, "bb", at, n)
            t = w * S["h"][at, wide(sz, n)]
            rt = rate_row(sz, S, k, n) * t
            s = sb if s is None else s + sb
            dd = rt if dd is None else dd + rt
            S["drate"][:, wide(sz, n)] = S["drate"][:, wide(sz, n)] + dt * t
            out.append(w)
        S["s"][at, :] = s
        S["dd"][at, :] = dd
        return tuple(out)

    lax.fori_loop(0, sz.L, body, start)


def finish(sz, S, k, g_ref):
    u, m, gy, dt = S["u"][...], S["m"][...], S["gy"][...], S["dt"][...]
    s = S["s"][...]
    dz = (u * s + S["dd"][...]) * m * jax.nn.sigmoid(S["z"][...])
    dp = mm(dz, S["dw"][k], ((1,), (1,)))
    col = lax.broadcasted_iota(jnp.int32, (LANES, LANES), 1)
    for n in range(sz.N):
        cut = slice(n * LANES, (n + 1) * LANES)
        dp = dp + mm(S["qb"][:, cut], (col == sz.R + n).astype(F32))
        dp = dp + mm(S["qc"][:, cut], (col == sz.R + sz.N + n).astype(F32))
    du = dt * s + S["skip"][k, 0:1, :] * gy + mm(dp, S["xw"][k], ((1,), (1,)))
    S["dv"][...] = S["dv"][...] + m * du
    at = sz.XR
    g_ref[k, :at, :] = mm(dp.T, u)[:at]
    g_ref[k, at : at + sz.DR, :] = mm(S["p"][...].T, dz)[: sz.DR]
    at += sz.DR
    g_ref[k, at : at + SUB, :] = jnp.zeros((SUB, sz.CP), F32)
    g_ref[k, at : at + 1, :] = jnp.sum(dz, axis=0, keepdims=True)
    g_ref[k, at + 1 : at + 2, :] = jnp.sum(gy * u, axis=0, keepdims=True)
    at += SUB
    for n in range(sz.N):
        total = jnp.sum(S["drate"][:, wide(sz, n)], axis=0, keepdims=True)
        g_ref[k, at + n : at + n + 1, :] = total * S["rate"][k * sz.N + n : k * sz.N + n + 1, :]


def place(sz):
    shape = (sz.L, SUB, sz.T)
    step, chunk, token = (lax.broadcasted_iota(jnp.int32, shape, axis) for axis in range(3))
    return (token == chunk * sz.L + step).astype(F32).reshape(sz.T, sz.T)


def row_inputs(sz, S, v_ref, t_ref):
    shape = (sz.L, SUB, sz.CP)
    step, chunk = (lax.broadcasted_iota(jnp.int32, shape, axis) for axis in range(2))
    token = (chunk * sz.L + step).reshape(sz.T, sz.CP)
    tiles = t_ref.shape[0]
    span = sz.T // tiles
    m = jnp.zeros((sz.T, sz.CP), F32)
    for w in range(tiles):
        inside = (token >= w * span) & (token < (w + 1) * span)
        m = jnp.where(inside, t_ref[w].astype(F32), m)
    S["m"][...] = m
    S["u"][...] = jnp.zeros_like(S["u"])
    S["u"][:, : sz.C] = mm(place(sz), v_ref[...])
    S["u"][...] = S["u"][...] * m


def rows_forward(sz, names, v_ref, t_ref, *rest):
    weights, out_ref, S = rest[:5], rest[5], dict(zip(names, rest[6:]))
    load_weights(sz, S, *weights)
    row_inputs(sz, S, v_ref, t_ref)
    S["y"][...] = jnp.zeros_like(S["y"])
    for k in range(2):
        prepare(sz, S, k)
        local_states(sz, S, k)
        run_states(sz, S, k, 0, edges(sz, S), True, True, False)
    lane = lax.broadcasted_iota(jnp.int32, (sz.T, sz.CP), 1)
    y = jnp.where(lane == sz.C, S["m"][...], S["y"][...])
    out_ref[...] = mm(place(sz), y, ((0,), (0,))).astype(BF)


def columns_both(sz, names, v_ref, c_ref, *rest):
    weights, out_ref, grad_ref, g_ref, S = rest[:5], rest[5], rest[6], rest[7], dict(zip(names, rest[8:]))
    load_weights(sz, S, *weights)
    v = v_ref[...].astype(F32)
    lane = lax.broadcasted_iota(jnp.int32, (sz.T, sz.CP), 1)
    m = jnp.broadcast_to(v[:, sz.C : sz.C + 1], (sz.T, sz.CP))
    S["m"][...] = m
    S["u"][...] = jnp.where(lane < sz.C, v, 0.0) * m
    S["gy"][...] = jnp.zeros_like(S["gy"])
    S["gy"][:, : sz.C] = c_ref[...].astype(F32)
    S["y"][...] = jnp.zeros_like(S["y"])
    S["dv"][...] = jnp.zeros_like(S["dv"])
    for k in range(2):
        prepare(sz, S, k)
        S["drate"][...] = jnp.zeros_like(S["drate"])

        def group_body(group, carry):
            run_states(sz, S, k, group, zeros(sz), False, True, True)
            run_adjoints(sz, S, k, group, zeros(sz))
            return carry

        lax.fori_loop(0, sz.M // SUB, group_body, 0)
        finish(sz, S, k, g_ref)
    out_ref[...] = S["y"][:, : sz.C].astype(BF)
    grad_ref[...] = S["dv"][...].astype(BF)


def rows_backward(sz, names, v_ref, t_ref, c_ref, *rest):
    weights, out_ref, g_ref, S = rest[:5], rest[5], rest[6], dict(zip(names, rest[7:]))
    load_weights(sz, S, *weights)
    row_inputs(sz, S, v_ref, t_ref)
    S["gy"][...] = mm(place(sz), c_ref[...])
    S["dv"][...] = jnp.zeros_like(S["dv"])
    for k in range(2):
        prepare(sz, S, k)
        S["drate"][...] = jnp.zeros_like(S["drate"])
        local_states(sz, S, k)
        run_states(sz, S, k, 0, edges(sz, S), True, False, True)
        local_adjoints(sz, S, k)
        run_adjoints(sz, S, k, 0, edges(sz, S))
        finish(sz, S, k, g_ref)
    out_ref[...] = mm(place(sz), S["dv"][...], ((0,), (0,)))[:, : sz.C].astype(BF)


def call(body, sz, out_shape, n_vmem_first, has_tissue, args, name):
    shapes = sz.scratch()
    specs = [pl.BlockSpec(memory_space=pltpu.VMEM)] * len(args)
    if has_tissue:
        specs[1] = pl.BlockSpec(memory_space=pltpu.SMEM)
    return pl.pallas_call(
        functools.partial(body, sz, tuple(shapes)),
        out_shape=out_shape,
        in_specs=specs,
        out_specs=jax.tree.map(lambda _: pl.BlockSpec(memory_space=pltpu.VMEM), out_shape),
        scratch_shapes=[pltpu.VMEM(shape, F32) for shape in shapes.values()],
        compiler_params=pltpu.CompilerParams(vmem_limit_bytes=56 * 1024 * 1024),
        name=name,
    )(*args)


def reduce_all(packed, axes):
    count = lax.axis_size(axes)
    size = packed.size
    each = up(size, count) // count
    flat = packed.reshape(-1)
    if each * count != size:
        flat = jnp.pad(flat, (0, each * count - size))
    parts = lax.all_to_all(flat.reshape(count, each), axes, split_axis=0, concat_axis=0, tiled=True)
    mine = jnp.broadcast_to(jnp.sum(parts, axis=0)[None], (count, each))
    gathered = lax.all_to_all(mine, axes, split_axis=0, concat_axis=0, tiled=True)
    return gathered.reshape(-1)[:size].reshape(packed.shape)


def shards(features, tissue, cotangent, x_proj, dt_proj, dt_bias, a_log, d_skip):
    local_slides, local_rows, width, channels = features.shape
    assert local_slides == 1 and local_rows == 1
    bands = lax.axis_size("band")
    cols = width // bands
    rank, states = dt_proj.shape[1], a_log.shape[1]
    weights = (x_proj, dt_proj, dt_bias, a_log, d_skip)
    horiz = tuple(weight[:2] for weight in weights)
    vert = tuple(weight[2:] for weight in weights)
    rz = Sizes(channels, rank, states, width // SUB, SUB)
    cz = Sizes(channels, rank, states, bands, cols)
    v = features.reshape(width, channels)
    t = tissue.reshape(-1)
    shape = jax.ShapeDtypeStruct
    carried = call(rows_forward, rz, shape((width, rz.CP), BF), 0, True, (v, t) + horiz, "rows_forward")
    moved = lax.all_to_all(carried.reshape(bands, cols, rz.CP), "band", split_axis=0, concat_axis=0, tiled=True)
    mixed, grad_cols, grads_v = call(
        columns_both, cz,
        (shape((cz.T, channels), BF), shape((cz.T, cz.CP), BF), shape((2, cz.rows, cz.CP), F32)),
        0, False, (moved.reshape(cz.T, cz.CP), cotangent.reshape(cz.T, channels)) + vert, "columns",
    )
    back = lax.all_to_all(grad_cols.reshape(bands, cols, cz.CP), "band", split_axis=0, concat_axis=0, tiled=True)
    grad_rows, grads_h = call(
        rows_backward, rz,
        (shape((width, channels), BF), shape((2, rz.rows, rz.CP), F32)),
        0, True, (v, t, back.reshape(width, rz.CP)) + horiz, "rows_backward",
    )
    packed = jnp.concatenate([grads_h, grads_v], axis=0)
    total = reduce_all(packed, ("slide", "band"))
    at = rz.XR + rz.DR
    return (
        mixed.reshape(cotangent.shape),
        grad_rows.reshape(features.shape),
        jnp.swapaxes(total[:, : rank + 2 * states, :channels], 1, 2),
        total[:, rz.XR : rz.XR + rank, :channels],
        total[:, at, :channels],
        total[:, at + SUB : at + SUB + states, :channels],
        total[:, at + 1, :channels],
    )


def solution(mesh):
    in_specs = (
        P(("groups", "slide"), "band", None, None),
        P(("groups", "slide"), "band", None),
        P(("groups", "slide"), None, "band", None),
        P(), P(), P(), P(), P(),
    )
    out_specs = (
        P(("groups", "slide"), None, "band", None),
        P(("groups", "slide"), "band", None, None),
        P("groups", None, None),
        P("groups", None, None),
        P("groups", None),
        P("groups", None, None),
        P("groups", None),
    )
    return jax.shard_map(shards, mesh=mesh, in_specs=in_specs, out_specs=out_specs, check_vma=False)
```

```python
import functools
import math

import jax
import jax.numpy as jnp
from jax import lax
from jax.experimental import pallas as pl
from jax.experimental.pallas import tpu as pltpu
from jax.sharding import PartitionSpec as P

BF = jnp.bfloat16
F32 = jnp.float32
SUB = 8
LANES = 128
LOG2E = math.log2(math.e)


def up(value, unit):
    return -(-value // unit) * unit


def mm(a, b, dims=((1,), (0,))):
    return lax.dot_general(a.astype(BF), b.astype(BF), (dims, ((), ())), preferred_element_type=F32)


def split(a):
    high = a.astype(BF)
    return high, (a - high.astype(F32)).astype(BF)


def mm_exact_left(a, b):
    high, low = split(b)
    return mm(a, high) + mm(a, low)


def mm_exact_right(a, b):
    high, low = split(a)
    return mm(high, b) + mm(low, b)


def mm_three(a, b):
    high, low = split(a)
    return mm_exact_left(high, b) + mm(low, b)


class Sizes:
    def __init__(self, channels, rank, states, steps, seqs):
        self.C, self.R, self.N = channels, rank, states
        self.CP = up(channels + 1, LANES)
        self.L, self.M = steps, seqs
        self.T = steps * seqs
        self.XR = up(rank + 2 * states, SUB)
        self.DR = up(rank, SUB)
        self.rows = up(self.XR + self.DR + SUB + up(states, SUB), 2 * SUB)

    def scratch(self):
        t, cp, n = self.T, self.CP, self.N
        wide, narrow = (t, n * cp), (t, n * LANES)
        shapes = dict(
            a=wide, h=wide, bb=narrow, cb=narrow, qb=narrow, qc=narrow,
            u=(t, cp), m=(t, cp), gy=(t, cp), dt=(t, cp), du=(t, cp), z=(t, cp), p=(t, LANES),
            y=(t, cp), s=(t, cp), dd=(t, cp), dv=(t, cp),
            xw=(2, cp, LANES), dw=(2, LANES, cp), bias=(2, SUB, cp), skip=(2, SUB, cp),
            rate=(2 * n, cp), drate=(SUB, n * cp), edge=(SUB, n * cp),
        )
        return shapes


def load_weights(sz, S, base, x_ref, d_ref, b_ref, l_ref, k_ref):
    for name in ("xw", "dw", "bias", "skip", "rate"):
        S[name][...] = jnp.zeros_like(S[name])
    for k in range(2):
        S["xw"][k, : sz.C, : sz.R + 2 * sz.N] = x_ref[base + k]
        S["dw"][k, : sz.R, : sz.C] = d_ref[base + k]
        S["bias"][k, :, : sz.C] = jnp.broadcast_to(b_ref[base + k : base + k + 1, :], (SUB, sz.C))
        S["skip"][k, :, : sz.C] = jnp.broadcast_to(k_ref[base + k : base + k + 1, :], (SUB, sz.C))
        S["rate"][k * sz.N : (k + 1) * sz.N, : sz.C] = -jnp.exp(l_ref[base + k])


def prepare(sz, S, k):
    u = S["u"][...]
    p = mm_exact_left(u, S["xw"][k])
    z = mm_three(p, S["dw"][k]) + S["bias"][k, 0:1, :]
    dt = (jnp.maximum(z, 0.0) + jnp.log1p(jnp.exp(-jnp.abs(z)))) * S["m"][...]
    S["p"][...] = p
    S["z"][...] = z
    S["dt"][...] = dt
    S["du"][...] = dt * u
    row = lax.broadcasted_iota(jnp.int32, (LANES, LANES), 0)
    for n in range(sz.N):
        cut = slice(n * LANES, (n + 1) * LANES)
        S["bb"][:, cut] = mm_exact_right(p, (row == sz.R + n).astype(F32))
        S["cb"][:, cut] = mm_exact_right(p, (row == sz.R + sz.N + n).astype(F32))


def wide(sz, n):
    return slice(n * sz.CP, (n + 1) * sz.CP)


def both(sz, value):
    return jnp.concatenate([value] * (sz.CP // LANES), axis=1)


def fold(sz, value):
    total = value[:, :LANES]
    for at in range(LANES, sz.CP, LANES):
        total = total + value[:, at : at + LANES]
    return total


def rows_of(sz, step, group, backwards):
    place = sz.L - 1 - step if backwards else step
    return pl.ds(pl.multiple_of(place * sz.M + group * SUB, SUB), SUB)


def rate_row(sz, S, k, n):
    return jnp.broadcast_to(S["rate"][k * sz.N + n : k * sz.N + n + 1, :], (SUB, sz.CP))


def b_of(sz, S, name, at, n):
    return both(sz, S[name][at, n * LANES : (n + 1) * LANES])


def shift(sz, value, backwards):
    row = lax.broadcasted_iota(jnp.int32, value.shape, 0)
    if backwards:
        return jnp.where(row == SUB - 1, 0.0, pltpu.roll(value, SUB - 1, 0))
    return jnp.where(row == 0, 0.0, pltpu.roll(value, 1, 0))


def join_chunks(sz, S, k, ends, backwards):
    total = jnp.zeros((SUB, sz.CP), F32)
    for step in range(sz.L):
        total = total + S["dt"][step * SUB : (step + 1) * SUB, :]
    for n in range(sz.N):
        decay = jnp.exp(total * rate_row(sz, S, k, n))
        start = jnp.zeros((SUB, sz.CP), F32)
        for _ in range(SUB - 1):
            start = shift(sz, decay * start + ends[n], backwards)
        S["edge"][:, wide(sz, n)] = start


def zeros(sz):
    return tuple(jnp.zeros((SUB, sz.CP), F32) for _ in range(sz.N))


def edges(sz, S):
    return tuple(S["edge"][:, wide(sz, n)] for n in range(sz.N))


def local_states(sz, S, k):
    rev = k == 1

    def body(i, h):
        at = rows_of(sz, i, 0, rev)
        dt, du = S["dt"][at, :], S["du"][at, :]
        out = []
        for n in range(sz.N):
            a = jnp.exp2(dt * (LOG2E * rate_row(sz, S, k, n)))
            S["a"][at, wide(sz, n)] = a
            out.append(a * h[n] + du * b_of(sz, S, "bb", at, n))
        return tuple(out)

    join_chunks(sz, S, k, lax.fori_loop(0, sz.L, body, zeros(sz)), rev)


def run_states(sz, S, k, group, start, chunked, want_y, want_grad):
    rev = k == 1

    def body(i, h):
        at = rows_of(sz, i, group, rev)
        dt, du = S["dt"][at, :], S["du"][at, :]
        gy = S["gy"][at, :] if want_grad else None
        y = None
        out = []
        for n in range(sz.N):
            if chunked:
                a = S["a"][at, wide(sz, n)]
            else:
                a = jnp.exp2(dt * (LOG2E * rate_row(sz, S, k, n)))
                S["a"][at, wide(sz, n)] = a
            new = a * h[n] + du * b_of(sz, S, "bb", at, n)
            if want_grad:
                S["h"][at, wide(sz, n)] = h[n]
                S["qc"][at, n * LANES : (n + 1) * LANES] = fold(sz, gy * new)
            if want_y:
                term = new * b_of(sz, S, "cb", at, n)
                y = term if y is None else y + term
            out.append(new)
        if want_y:
            S["y"][at, :] = S["y"][at, :] + y + S["skip"][k] * S["u"][at, :]
        return tuple(out)

    lax.fori_loop(0, sz.L, body, start)


def local_adjoints(sz, S, k):
    rev = k == 0

    def body(i, e):
        at = rows_of(sz, i, 0, rev)
        gy = S["gy"][at, :]
        return tuple(
            S["a"][at, wide(sz, n)] * (b_of(sz, S, "cb", at, n) * gy + e[n]) for n in range(sz.N)
        )

    join_chunks(sz, S, k, lax.fori_loop(0, sz.L, body, zeros(sz)), rev)


def run_adjoints(sz, S, k, group, start):
    rev = k == 0

    def body(i, e):
        at = rows_of(sz, i, group, rev)
        gy, dt, du = S["gy"][at, :], S["dt"][at, :], S["du"][at, :]
        s = dd = None
        out = []
        for n in range(sz.N):
            g = b_of(sz, S, "cb", at, n) * gy + e[n]
            w = S["a"][at, wide(sz, n)] * g
            S["qb"][at, n * LANES : (n + 1) * LANES] = fold(sz, g * du)
            sb = g * b_of(sz, S, "bb", at, n)
            t = w * S["h"][at, wide(sz, n)]
            rt = rate_row(sz, S, k, n) * t
            s = sb if s is None else s + sb
            dd = rt if dd is None else dd + rt
            S["drate"][:, wide(sz, n)] = S["drate"][:, wide(sz, n)] + dt * t
            out.append(w)
        S["s"][at, :] = s
        S["dd"][at, :] = dd
        return tuple(out)

    lax.fori_loop(0, sz.L, body, start)


def finish(sz, S, k, g_ref):
    u, m, gy, dt = S["u"][...], S["m"][...], S["gy"][...], S["dt"][...]
    s = S["s"][...]
    dz = (u * s + S["dd"][...]) * m * jax.nn.sigmoid(S["z"][...])
    dp = mm(dz, S["dw"][k], ((1,), (1,)))
    col = lax.broadcasted_iota(jnp.int32, (LANES, LANES), 1)
    for n in range(sz.N):
        cut = slice(n * LANES, (n + 1) * LANES)
        dp = dp + mm(S["qb"][:, cut], (col == sz.R + n).astype(F32))
        dp = dp + mm(S["qc"][:, cut], (col == sz.R + sz.N + n).astype(F32))
    du = dt * s + S["skip"][k, 0:1, :] * gy + mm(dp, S["xw"][k], ((1,), (1,)))
    S["dv"][...] = S["dv"][...] + m * du
    at = sz.XR
    g_ref[k, :, :] = jnp.zeros((sz.rows, sz.CP), F32)
    g_ref[k, :at, :] = mm(dp.T, u)[:at]
    g_ref[k, at : at + sz.DR, :] = mm(S["p"][...].T, dz)[: sz.DR]
    at += sz.DR
    g_ref[k, at : at + 1, :] = jnp.sum(dz, axis=0, keepdims=True)
    g_ref[k, at + 1 : at + 2, :] = jnp.sum(gy * u, axis=0, keepdims=True)
    at += SUB
    for n in range(sz.N):
        total = jnp.sum(S["drate"][:, wide(sz, n)], axis=0, keepdims=True)
        g_ref[k, at + n : at + n + 1, :] = total * S["rate"][k * sz.N + n : k * sz.N + n + 1, :]


def place(sz):
    shape = (sz.L, SUB, sz.T)
    step, chunk, token = (lax.broadcasted_iota(jnp.int32, shape, axis) for axis in range(3))
    return (token == chunk * sz.L + step).astype(F32).reshape(sz.T, sz.T)


def row_inputs(sz, S, v_ref, t_ref):
    shape = (sz.L, SUB, sz.CP)
    step, chunk = (lax.broadcasted_iota(jnp.int32, shape, axis) for axis in range(2))
    token = (chunk * sz.L + step).reshape(sz.T, sz.CP)
    tiles = t_ref.shape[0]
    span = sz.T // tiles
    m = jnp.zeros((sz.T, sz.CP), F32)
    for w in range(tiles):
        inside = (token >= w * span) & (token < (w + 1) * span)
        m = jnp.where(inside, t_ref[w].astype(F32), m)
    S["m"][...] = m
    S["u"][...] = jnp.zeros_like(S["u"])
    S["u"][:, : sz.C] = mm(place(sz), v_ref[...])
    S["u"][...] = S["u"][...] * m


def rows_forward(sz, names, v_ref, t_ref, *rest):
    weights, out_ref, S = rest[:5], rest[5], dict(zip(names, rest[6:]))
    load_weights(sz, S, 0, *weights)
    row_inputs(sz, S, v_ref, t_ref)
    S["y"][...] = jnp.zeros_like(S["y"])
    for k in range(2):
        prepare(sz, S, k)
        local_states(sz, S, k)
        run_states(sz, S, k, 0, edges(sz, S), True, True, False)
    lane = lax.broadcasted_iota(jnp.int32, (sz.T, sz.CP), 1)
    y = jnp.where(lane == sz.C, S["m"][...], S["y"][...])
    out_ref[...] = mm(place(sz), y, ((0,), (0,))).astype(BF)


def columns_both(sz, names, v_ref, c_ref, *rest):
    weights, out_ref, grad_ref, g_ref, S = rest[:5], rest[5], rest[6], rest[7], dict(zip(names, rest[8:]))
    load_weights(sz, S, 2, *weights)
    v = v_ref[...].astype(F32)
    lane = lax.broadcasted_iota(jnp.int32, (sz.T, sz.CP), 1)
    m = jnp.broadcast_to(v[:, sz.C : sz.C + 1], (sz.T, sz.CP))
    S["m"][...] = m
    S["u"][...] = jnp.where(lane < sz.C, v, 0.0) * m
    S["gy"][...] = jnp.zeros_like(S["gy"])
    S["gy"][:, : sz.C] = c_ref[...].astype(F32)
    S["y"][...] = jnp.zeros_like(S["y"])
    S["dv"][...] = jnp.zeros_like(S["dv"])
    for k in range(2):
        prepare(sz, S, k)
        S["drate"][...] = jnp.zeros_like(S["drate"])

        def group_body(group, carry):
            run_states(sz, S, k, group, zeros(sz), False, True, True)
            run_adjoints(sz, S, k, group, zeros(sz))
            return carry

        lax.fori_loop(0, sz.M // SUB, group_body, 0)
        finish(sz, S, k, g_ref)
    out_ref[...] = S["y"][:, : sz.C].astype(BF)
    grad_ref[...] = S["dv"][...].astype(BF)


def rows_backward(sz, names, v_ref, t_ref, c_ref, *rest):
    weights, out_ref, g_ref, S = rest[:5], rest[5], rest[6], dict(zip(names, rest[7:]))
    load_weights(sz, S, 0, *weights)
    row_inputs(sz, S, v_ref, t_ref)
    S["gy"][...] = mm(place(sz), c_ref[...])
    S["dv"][...] = jnp.zeros_like(S["dv"])
    for k in range(2):
        prepare(sz, S, k)
        S["drate"][...] = jnp.zeros_like(S["drate"])
        local_states(sz, S, k)
        run_states(sz, S, k, 0, edges(sz, S), True, False, True)
        local_adjoints(sz, S, k)
        run_adjoints(sz, S, k, 0, edges(sz, S))
        finish(sz, S, k, g_ref)
    out_ref[...] = mm(place(sz), S["dv"][...], ((0,), (0,)))[:, : sz.C].astype(BF)


def call(body, sz, out_shape, n_vmem_first, has_tissue, args, name):
    shapes = sz.scratch()
    specs = [pl.BlockSpec(memory_space=pltpu.VMEM)] * len(args)
    if has_tissue:
        specs[1] = pl.BlockSpec(memory_space=pltpu.SMEM)
    return pl.pallas_call(
        functools.partial(body, sz, tuple(shapes)),
        out_shape=out_shape,
        in_specs=specs,
        out_specs=jax.tree.map(lambda _: pl.BlockSpec(memory_space=pltpu.VMEM), out_shape),
        scratch_shapes=[pltpu.VMEM(shape, F32) for shape in shapes.values()],
        compiler_params=pltpu.CompilerParams(vmem_limit_bytes=56 * 1024 * 1024),
        name=name,
    )(*args)


def greet(sides):
    barrier = pltpu.get_barrier_semaphore()
    total = 0
    for axis, count in sides:
        me = lax.axis_index(axis)
        for off in range(1, count):
            pl.semaphore_signal(
                barrier, inc=1, device_id={axis: lax.rem(me + off, count)},
                device_id_type=pl.DeviceIdType.MESH,
            )
        total += count - 1
    pl.semaphore_wait(barrier, total)


def spread(axis, count, source_of, land, send_sem, recv_sem):
    me = lax.axis_index(axis)
    copies = []
    for off in range(1, count):
        other = lax.rem(me + off, count)
        copies.append(
            pltpu.make_async_remote_copy(
                src_ref=source_of(other), dst_ref=land.at[me],
                send_sem=send_sem.at[off], recv_sem=recv_sem.at[off],
                device_id={axis: other}, device_id_type=pl.DeviceIdType.MESH,
            )
        )
    for copy in copies:
        copy.start()
    return copies


def exchange_body(count, in_ref, out_ref, land, send_sem, recv_sem):
    greet((("band", count),))
    me = lax.axis_index("band")
    copies = spread("band", count, lambda other: in_ref.at[other], land, send_sem, recv_sem)
    land[me] = in_ref[me]
    for copy in copies:
        copy.wait()
    out_ref[...] = land[...]


def exchange(blocks, ident):
    count = lax.axis_size("band")
    return pl.pallas_call(
        functools.partial(exchange_body, count),
        out_shape=jax.ShapeDtypeStruct(blocks.shape, blocks.dtype),
        in_specs=[pl.BlockSpec(memory_space=pltpu.VMEM)],
        out_specs=pl.BlockSpec(memory_space=pltpu.VMEM),
        scratch_shapes=[
            pltpu.VMEM(blocks.shape, blocks.dtype),
            pltpu.SemaphoreType.DMA((count,)),
            pltpu.SemaphoreType.DMA((count,)),
        ],
        compiler_params=pltpu.CompilerParams(collective_id=ident, has_side_effects=True),
        name="band_exchange",
    )(blocks)


def reduce_body(slides, bands, each, h_ref, v_ref, out_ref, pack, land, part, every, total, whole, *sems):
    greet((("slide", slides), ("band", bands)))
    slide, band = lax.axis_index("slide"), lax.axis_index("band")
    rows = h_ref.shape[1]
    flat = 2 * h_ref.shape[0] * rows
    values = [ref[k] for ref in (h_ref, v_ref) for k in range(ref.shape[0])]
    spare = slides * each - flat
    if spare:
        values.append(jnp.zeros((spare, h_ref.shape[2]), F32))
    pack[...] = jnp.concatenate(values, axis=0).astype(BF).reshape(pack.shape)
    copies = spread("slide", slides, lambda other: pack.at[other], land, sems[0], sems[1])
    land[slide] = pack[slide]
    for copy in copies:
        copy.wait()
    part[...] = sum(land[at].astype(F32) for at in range(slides)).astype(BF)
    copies = spread("band", bands, lambda other: part, every, sems[2], sems[3])
    every[band] = part[...]
    for copy in copies:
        copy.wait()
    total[...] = sum(every[at].astype(F32) for at in range(bands)).astype(BF)
    copies = spread("slide", slides, lambda other: total, whole, sems[4], sems[5])
    whole[slide] = total[...]
    for copy in copies:
        copy.wait()
    out_ref[...] = whole[...].astype(F32)


def reduce_all(grads_h, grads_v):
    slides, bands = lax.axis_size("slide"), lax.axis_size("band")
    half, rows, lanes = grads_h.shape
    each = up(up(2 * half * rows, slides) // slides, 2 * SUB)
    block = (each, lanes)
    out = pl.pallas_call(
        functools.partial(reduce_body, slides, bands, each),
        out_shape=jax.ShapeDtypeStruct((slides,) + block, F32),
        in_specs=[pl.BlockSpec(memory_space=pltpu.VMEM)] * 2,
        out_specs=pl.BlockSpec(memory_space=pltpu.VMEM),
        scratch_shapes=[
            pltpu.VMEM((slides,) + block, BF), pltpu.VMEM((slides,) + block, BF),
            pltpu.VMEM(block, BF), pltpu.VMEM((bands,) + block, BF),
            pltpu.VMEM(block, BF), pltpu.VMEM((slides,) + block, BF),
        ]
        + [pltpu.SemaphoreType.DMA((count,)) for count in (slides, slides, bands, bands, slides, slides)],
        compiler_params=pltpu.CompilerParams(
            collective_id=2, has_side_effects=True, vmem_limit_bytes=32 * 1024 * 1024
        ),
        name="gradient_sum",
    )(grads_h, grads_v)
    return out.reshape(slides * each, lanes)[: 2 * half * rows].reshape(2 * half, rows, lanes)


def shards(features, tissue, cotangent, x_proj, dt_proj, dt_bias, a_log, d_skip):
    local_slides, local_rows, width, channels = features.shape
    assert local_slides == 1 and local_rows == 1
    bands = lax.axis_size("band")
    cols = width // bands
    rank, states = dt_proj.shape[1], a_log.shape[1]
    weights = (x_proj, dt_proj, dt_bias, a_log, d_skip)
    rz = Sizes(channels, rank, states, width // SUB, SUB)
    cz = Sizes(channels, rank, states, bands, cols)
    v = features.reshape(width, channels)
    t = tissue.reshape(-1)
    shape = jax.ShapeDtypeStruct
    carried = call(rows_forward, rz, shape((width, rz.CP), BF), 0, True, (v, t) + weights, "rows_forward")
    moved = exchange(carried.reshape(bands, cols, rz.CP), 0)
    mixed, grad_cols, grads_v = call(
        columns_both, cz,
        (shape((cz.T, channels), BF), shape((cz.T, cz.CP), BF), shape((2, cz.rows, cz.CP), F32)),
        0, False, (moved.reshape(cz.T, cz.CP), cotangent.reshape(cz.T, channels)) + weights, "columns",
    )
    back = exchange(grad_cols.reshape(bands, cols, cz.CP), 1)
    grad_rows, grads_h = call(
        rows_backward, rz,
        (shape((width, channels), BF), shape((2, rz.rows, rz.CP), F32)),
        0, True, (v, t, back.reshape(width, rz.CP)) + weights, "rows_backward",
    )
    total = reduce_all(grads_h, grads_v)
    at = rz.XR + rz.DR
    return (
        mixed.reshape(cotangent.shape),
        grad_rows.reshape(features.shape),
        jnp.swapaxes(total[:, : rank + 2 * states, :channels], 1, 2),
        total[:, rz.XR : rz.XR + rank, :channels],
        total[:, at, :channels],
        total[:, at + SUB : at + SUB + states, :channels],
        total[:, at + 1, :channels],
    )


def solution(mesh):
    in_specs = (
        P(("groups", "slide"), "band", None, None),
        P(("groups", "slide"), "band", None),
        P(("groups", "slide"), None, "band", None),
        P(), P(), P(), P(), P(),
    )
    out_specs = (
        P(("groups", "slide"), None, "band", None),
        P(("groups", "slide"), "band", None, None),
        P("groups", None, None),
        P("groups", None, None),
        P("groups", None),
        P("groups", None, None),
        P("groups", None),
    )
    return jax.shard_map(shards, mesh=mesh, in_specs=in_specs, out_specs=out_specs, check_vma=False)
```

```python
import functools
import math

import jax
import jax.numpy as jnp
from jax import lax
from jax.experimental import pallas as pl
from jax.experimental.pallas import tpu as pltpu
from jax.sharding import PartitionSpec as P

BF = jnp.bfloat16
F32 = jnp.float32
SUB = 8
LANES = 128
LOG2E = math.log2(math.e)


def up(value, unit):
    return -(-value // unit) * unit


def mm(a, b, dims=((1,), (0,))):
    return lax.dot_general(a.astype(BF), b.astype(BF), (dims, ((), ())), preferred_element_type=F32)


def split(a):
    high = a.astype(BF)
    return high, (a - high.astype(F32)).astype(BF)


def mm_exact_left(a, b):
    high, low = split(b)
    return mm(a, high) + mm(a, low)


def mm_exact_right(a, b):
    high, low = split(a)
    return mm(high, b) + mm(low, b)


def mm_three(a, b):
    high, low = split(a)
    return mm_exact_left(high, b) + mm(low, b)


class Sizes:
    def __init__(self, channels, rank, states, steps, seqs):
        self.C, self.R, self.N = channels, rank, states
        self.CP = up(channels + 1, LANES)
        self.L, self.M = steps, seqs
        self.T = steps * seqs
        self.XR = up(rank + 2 * states, SUB)
        self.DR = up(rank, SUB)
        self.rows = up(self.XR + self.DR + SUB + up(states, SUB), 2 * SUB)

    def scratch(self):
        t, cp, n = self.T, self.CP, self.N
        wide, narrow = (t, n * cp), (t, n * LANES)
        shapes = dict(
            a=wide, h=wide, bb=narrow, cb=narrow, qb=narrow, qc=narrow,
            u=(t, cp), m=(t, cp), gy=(t, cp), dt=(t, cp), du=(t, cp), z=(t, cp), p=(t, LANES),
            y=(t, cp), s=(t, cp), dd=(t, cp), dv=(t, cp),
            xw=(2, cp, LANES), dw=(2, LANES, cp), bias=(2, SUB, cp), skip=(2, SUB, cp),
            rate=(2 * n, cp), drate=(SUB, n * cp), edge=(SUB, n * cp),
        )
        return shapes


def load_weights(sz, S, base, x_ref, d_ref, b_ref, l_ref, k_ref):
    for name in ("xw", "dw", "bias", "skip", "rate"):
        S[name][...] = jnp.zeros_like(S[name])
    for k in range(2):
        S["xw"][k, : sz.C, : sz.R + 2 * sz.N] = x_ref[base + k]
        S["dw"][k, : sz.R, : sz.C] = d_ref[base + k]
        S["bias"][k, :, : sz.C] = jnp.broadcast_to(b_ref[base + k : base + k + 1, :], (SUB, sz.C))
        S["skip"][k, :, : sz.C] = jnp.broadcast_to(k_ref[base + k : base + k + 1, :], (SUB, sz.C))
        S["rate"][k * sz.N : (k + 1) * sz.N, : sz.C] = -jnp.exp(l_ref[base + k])


def prepare(sz, S, k):
    u = S["u"][...]
    p = mm_exact_left(u, S["xw"][k])
    z = mm_three(p, S["dw"][k]) + S["bias"][k, 0:1, :]
    dt = (jnp.maximum(z, 0.0) + jnp.log1p(jnp.exp(-jnp.abs(z)))) * S["m"][...]
    S["p"][...] = p
    S["z"][...] = z
    S["dt"][...] = dt
    S["du"][...] = dt * u
    row = lax.broadcasted_iota(jnp.int32, (LANES, LANES), 0)
    for n in range(sz.N):
        cut = slice(n * LANES, (n + 1) * LANES)
        S["bb"][:, cut] = mm_exact_right(p, (row == sz.R + n).astype(F32))
        S["cb"][:, cut] = mm_exact_right(p, (row == sz.R + sz.N + n).astype(F32))


def wide(sz, n):
    return slice(n * sz.CP, (n + 1) * sz.CP)


def both(sz, value):
    return jnp.concatenate([value] * (sz.CP // LANES), axis=1)


def fold(sz, value):
    total = value[:, :LANES]
    for at in range(LANES, sz.CP, LANES):
        total = total + value[:, at : at + LANES]
    return total


def rows_of(sz, step, group, backwards):
    place = sz.L - 1 - step if backwards else step
    return pl.ds(pl.multiple_of(place * sz.M + group * SUB, SUB), SUB)


def rate_row(sz, S, k, n):
    return jnp.broadcast_to(S["rate"][k * sz.N + n : k * sz.N + n + 1, :], (SUB, sz.CP))


def b_of(sz, S, name, at, n):
    return both(sz, S[name][at, n * LANES : (n + 1) * LANES])


def shift(sz, value, backwards):
    row = lax.broadcasted_iota(jnp.int32, value.shape, 0)
    if backwards:
        return jnp.where(row == SUB - 1, 0.0, pltpu.roll(value, SUB - 1, 0))
    return jnp.where(row == 0, 0.0, pltpu.roll(value, 1, 0))


def join_chunks(sz, S, k, ends, backwards):
    total = jnp.zeros((SUB, sz.CP), F32)
    for step in range(sz.L):
        total = total + S["dt"][step * SUB : (step + 1) * SUB, :]
    for n in range(sz.N):
        decay = jnp.exp(total * rate_row(sz, S, k, n))
        start = jnp.zeros((SUB, sz.CP), F32)
        for _ in range(SUB - 1):
            start = shift(sz, decay * start + ends[n], backwards)
        S["edge"][:, wide(sz, n)] = start


def zeros(sz):
    return tuple(jnp.zeros((SUB, sz.CP), F32) for _ in range(sz.N))


def edges(sz, S):
    return tuple(S["edge"][:, wide(sz, n)] for n in range(sz.N))


def local_states(sz, S, k):
    rev = k == 1

    def body(i, h):
        at = rows_of(sz, i, 0, rev)
        dt, du = S["dt"][at, :], S["du"][at, :]
        out = []
        for n in range(sz.N):
            a = jnp.exp2(dt * (LOG2E * rate_row(sz, S, k, n)))
            S["a"][at, wide(sz, n)] = a
            out.append(a * h[n] + du * b_of(sz, S, "bb", at, n))
        return tuple(out)

    join_chunks(sz, S, k, lax.fori_loop(0, sz.L, body, zeros(sz)), rev)


def run_states(sz, S, k, group, start, chunked, want_y, want_grad):
    rev = k == 1

    def body(i, h):
        at = rows_of(sz, i, group, rev)
        dt, du = S["dt"][at, :], S["du"][at, :]
        gy = S["gy"][at, :] if want_grad else None
        y = None
        out = []
        for n in range(sz.N):
            if chunked:
                a = S["a"][at, wide(sz, n)]
            else:
                a = jnp.exp2(dt * (LOG2E * rate_row(sz, S, k, n)))
                S["a"][at, wide(sz, n)] = a
            new = a * h[n] + du * b_of(sz, S, "bb", at, n)
            if want_grad:
                S["h"][at, wide(sz, n)] = h[n]
                S["qc"][at, n * LANES : (n + 1) * LANES] = fold(sz, gy * new)
            if want_y:
                term = new * b_of(sz, S, "cb", at, n)
                y = term if y is None else y + term
            out.append(new)
        if want_y:
            S["y"][at, :] = S["y"][at, :] + y + S["skip"][k] * S["u"][at, :]
        return tuple(out)

    lax.fori_loop(0, sz.L, body, start)


def local_adjoints(sz, S, k):
    rev = k == 0

    def body(i, e):
        at = rows_of(sz, i, 0, rev)
        gy = S["gy"][at, :]
        return tuple(
            S["a"][at, wide(sz, n)] * (b_of(sz, S, "cb", at, n) * gy + e[n]) for n in range(sz.N)
        )

    join_chunks(sz, S, k, lax.fori_loop(0, sz.L, body, zeros(sz)), rev)


def run_adjoints(sz, S, k, group, start):
    rev = k == 0

    def body(i, e):
        at = rows_of(sz, i, group, rev)
        gy, dt, du = S["gy"][at, :], S["dt"][at, :], S["du"][at, :]
        s = dd = None
        out = []
        for n in range(sz.N):
            g = b_of(sz, S, "cb", at, n) * gy + e[n]
            w = S["a"][at, wide(sz, n)] * g
            S["qb"][at, n * LANES : (n + 1) * LANES] = fold(sz, g * du)
            sb = g * b_of(sz, S, "bb", at, n)
            t = w * S["h"][at, wide(sz, n)]
            rt = rate_row(sz, S, k, n) * t
            s = sb if s is None else s + sb
            dd = rt if dd is None else dd + rt
            S["drate"][:, wide(sz, n)] = S["drate"][:, wide(sz, n)] + dt * t
            out.append(w)
        S["s"][at, :] = s
        S["dd"][at, :] = dd
        return tuple(out)

    lax.fori_loop(0, sz.L, body, start)


def finish(sz, S, k, g_ref):
    u, m, gy, dt = S["u"][...], S["m"][...], S["gy"][...], S["dt"][...]
    s = S["s"][...]
    dz = (u * s + S["dd"][...]) * m * jax.nn.sigmoid(S["z"][...])
    dp = mm(dz, S["dw"][k], ((1,), (1,)))
    col = lax.broadcasted_iota(jnp.int32, (LANES, LANES), 1)
    for n in range(sz.N):
        cut = slice(n * LANES, (n + 1) * LANES)
        dp = dp + mm(S["qb"][:, cut], (col == sz.R + n).astype(F32))
        dp = dp + mm(S["qc"][:, cut], (col == sz.R + sz.N + n).astype(F32))
    du = dt * s + S["skip"][k, 0:1, :] * gy + mm(dp, S["xw"][k], ((1,), (1,)))
    S["dv"][...] = S["dv"][...] + m * du
    at = sz.XR
    g_ref[k, :, :] = jnp.zeros((sz.rows, sz.CP), F32)
    g_ref[k, :at, :] = mm(dp.T, u)[:at]
    g_ref[k, at : at + sz.DR, :] = mm(S["p"][...].T, dz)[: sz.DR]
    at += sz.DR
    g_ref[k, at : at + 1, :] = jnp.sum(dz, axis=0, keepdims=True)
    g_ref[k, at + 1 : at + 2, :] = jnp.sum(gy * u, axis=0, keepdims=True)
    at += SUB
    for n in range(sz.N):
        total = jnp.sum(S["drate"][:, wide(sz, n)], axis=0, keepdims=True)
        g_ref[k, at + n : at + n + 1, :] = total * S["rate"][k * sz.N + n : k * sz.N + n + 1, :]


def place(sz):
    shape = (sz.L, SUB, sz.T)
    step, chunk, token = (lax.broadcasted_iota(jnp.int32, shape, axis) for axis in range(3))
    return (token == chunk * sz.L + step).astype(F32).reshape(sz.T, sz.T)


def row_inputs(sz, S, v_ref, t_ref):
    shape = (sz.L, SUB, sz.CP)
    step, chunk = (lax.broadcasted_iota(jnp.int32, shape, axis) for axis in range(2))
    token = (chunk * sz.L + step).reshape(sz.T, sz.CP)
    tiles = t_ref.shape[0]
    span = sz.T // tiles
    m = jnp.zeros((sz.T, sz.CP), F32)
    for w in range(tiles):
        inside = (token >= w * span) & (token < (w + 1) * span)
        m = jnp.where(inside, t_ref[w].astype(F32), m)
    S["m"][...] = m
    S["u"][...] = jnp.zeros_like(S["u"])
    S["u"][:, : sz.C] = mm(place(sz), v_ref[...], ((1,), (1,)))
    S["u"][...] = S["u"][...] * m


def greet(sides):
    barrier = pltpu.get_barrier_semaphore()
    total = 0
    for axis, count in sides:
        me = lax.axis_index(axis)
        for off in range(1, count):
            pl.semaphore_signal(
                barrier, inc=1, device_id={axis: lax.rem(me + off, count)},
                device_id_type=pl.DeviceIdType.MESH,
            )
        total += count - 1
    return lambda: pl.semaphore_wait(barrier, total)


def spread(axis, count, source_of, land, send_sem, recv_sem):
    me = lax.axis_index(axis)
    copies = []
    for off in range(1, count):
        other = lax.rem(me + off, count)
        copies.append(
            pltpu.make_async_remote_copy(
                src_ref=source_of(other), dst_ref=land.at[me],
                send_sem=send_sem.at[off], recv_sem=recv_sem.at[off],
                device_id={axis: other}, device_id_type=pl.DeviceIdType.MESH,
            )
        )
    for copy in copies:
        copy.start()
    return copies


def sum_gradients(slides, bands, each, h_ref, v_ref, out_ref, pack, land, part, every, total, whole, *sems):
    slide, band = lax.axis_index("slide"), lax.axis_index("band")
    rows = h_ref.shape[1]
    flat = 2 * h_ref.shape[0] * rows
    values = [ref[k] for ref in (h_ref, v_ref) for k in range(ref.shape[0])]
    spare = slides * each - flat
    if spare:
        values.append(jnp.zeros((spare, h_ref.shape[2]), F32))
    pack[...] = jnp.concatenate(values, axis=0).astype(BF).reshape(pack.shape)
    copies = spread("slide", slides, lambda other: pack.at[other], land, sems[0], sems[1])
    land[slide] = pack[slide]
    for copy in copies:
        copy.wait()
    part[...] = sum(land[at].astype(F32) for at in range(slides)).astype(BF)
    copies = spread("band", bands, lambda other: part, every, sems[2], sems[3])
    every[band] = part[...]
    for copy in copies:
        copy.wait()
    total[...] = sum(every[at].astype(F32) for at in range(bands)).astype(BF)
    copies = spread("slide", slides, lambda other: total, whole, sems[4], sems[5])
    whole[slide] = total[...]
    for copy in copies:
        copy.wait()
    out_ref[...] = whole[...].astype(F32)


def rows_forward(bands, sz, names, v_ref, t_ref, *rest):
    weights, out_ref, S = rest[:5], rest[5], dict(zip(names, rest[6:]))
    block, land, send_sem, recv_sem = rest[6 + len(names) :]
    arrived = greet((("band", bands),))
    load_weights(sz, S, 0, *weights)
    row_inputs(sz, S, v_ref, t_ref)
    S["y"][...] = jnp.zeros_like(S["y"])
    for k in range(2):
        prepare(sz, S, k)
        local_states(sz, S, k)
        run_states(sz, S, k, 0, edges(sz, S), True, True, False)
    lane = lax.broadcasted_iota(jnp.int32, (sz.T, sz.CP), 1)
    y = jnp.where(lane == sz.C, S["m"][...], S["y"][...])
    block[...] = mm(place(sz), y, ((0,), (0,))).astype(BF).reshape(block.shape)
    arrived()
    me = lax.axis_index("band")
    copies = spread("band", bands, lambda other: block.at[other], land, send_sem, recv_sem)
    land[me] = block[me]
    for copy in copies:
        copy.wait()
    out_ref[...] = land[...]


def columns_both(sz, names, v_ref, c_ref, *rest):
    weights, out_ref, grad_ref, g_ref, S = rest[:5], rest[5], rest[6], rest[7], dict(zip(names, rest[8:]))
    load_weights(sz, S, 2, *weights)
    v = v_ref[...].astype(F32)
    lane = lax.broadcasted_iota(jnp.int32, (sz.T, sz.CP), 1)
    m = jnp.broadcast_to(v[:, sz.C : sz.C + 1], (sz.T, sz.CP))
    S["m"][...] = m
    S["u"][...] = jnp.where(lane < sz.C, v, 0.0) * m
    S["gy"][...] = jnp.zeros_like(S["gy"])
    S["gy"][:, : sz.C] = c_ref[...].astype(F32)
    S["y"][...] = jnp.zeros_like(S["y"])
    S["dv"][...] = jnp.zeros_like(S["dv"])
    for k in range(2):
        prepare(sz, S, k)
        S["drate"][...] = jnp.zeros_like(S["drate"])

        def group_body(group, carry):
            run_states(sz, S, k, group, zeros(sz), False, True, True)
            run_adjoints(sz, S, k, group, zeros(sz))
            return carry

        lax.fori_loop(0, sz.M // SUB, group_body, 0)
        finish(sz, S, k, g_ref)
    out_ref[...] = S["y"][:, : sz.C].astype(BF)
    grad_ref[...] = S["dv"][...].astype(BF)


def rows_backward(slides, bands, each, sz, names, v_ref, t_ref, c_ref, gv_ref, *rest):
    weights, out_ref, sum_ref, S = rest[:5], rest[5], rest[6], dict(zip(names, rest[7:]))
    land, send_sem, recv_sem, g_ref, *summing = rest[7 + len(names) :]
    arrived = greet((("slide", slides), ("band", bands)))
    load_weights(sz, S, 0, *weights)
    row_inputs(sz, S, v_ref, t_ref)
    S["dv"][...] = jnp.zeros_like(S["dv"])
    arrived()
    me = lax.axis_index("band")
    copies = spread("band", bands, lambda other: c_ref.at[other], land, send_sem, recv_sem)
    land[me] = c_ref[me]
    for k in range(2):
        prepare(sz, S, k)
        S["drate"][...] = jnp.zeros_like(S["drate"])
        local_states(sz, S, k)
        if k == 0:
            for copy in copies:
                copy.wait()
            S["gy"][...] = mm(place(sz), land[...].reshape(sz.T, sz.CP))
        run_states(sz, S, k, 0, edges(sz, S), True, False, True)
        local_adjoints(sz, S, k)
        run_adjoints(sz, S, k, 0, edges(sz, S))
        finish(sz, S, k, g_ref)
    out_ref[...] = mm(S["dv"][...], place(sz), ((0,), (0,)))[: sz.C].astype(BF)
    sum_gradients(slides, bands, each, g_ref, gv_ref, sum_ref, *summing)


def call(body, sz, out_shape, has_tissue, args, name, extra=(), ident=None):
    shapes = sz.scratch()
    specs = [pl.BlockSpec(memory_space=pltpu.VMEM)] * len(args)
    if has_tissue:
        specs[1] = pl.BlockSpec(memory_space=pltpu.SMEM)
    return pl.pallas_call(
        functools.partial(body, sz, tuple(shapes)),
        out_shape=out_shape,
        in_specs=specs,
        out_specs=jax.tree.map(lambda _: pl.BlockSpec(memory_space=pltpu.VMEM), out_shape),
        scratch_shapes=[pltpu.VMEM(shape, F32) for shape in shapes.values()] + list(extra),
        compiler_params=pltpu.CompilerParams(
            vmem_limit_bytes=56 * 1024 * 1024, collective_id=ident, has_side_effects=ident is not None
        ),
        name=name,
    )(*args)


def shards(features, tissue, cotangent, x_proj, dt_proj, dt_bias, a_log, d_skip):
    local_slides, local_rows, width, channels = features.shape
    assert local_slides == 1 and local_rows == 1
    bands = lax.axis_size("band")
    cols = width // bands
    rank, states = dt_proj.shape[1], a_log.shape[1]
    weights = (x_proj, dt_proj, dt_bias, a_log, d_skip)
    rz = Sizes(channels, rank, states, width // SUB, SUB)
    cz = Sizes(channels, rank, states, bands, cols)
    v = jnp.swapaxes(features.reshape(width, channels), 0, 1)
    t = tissue.reshape(-1)
    shape = jax.ShapeDtypeStruct
    slides = lax.axis_size("slide")
    moved_shape = (bands, cols, rz.CP)
    dma = pltpu.SemaphoreType.DMA
    moved = call(
        functools.partial(rows_forward, bands), rz, shape(moved_shape, BF), True, (v, t) + weights, "rows_forward",
        [pltpu.VMEM(moved_shape, BF), pltpu.VMEM(moved_shape, BF), dma((bands,)), dma((bands,))], 0,
    )
    mixed, grad_cols, grads_v = call(
        columns_both, cz,
        (shape((cz.T, channels), BF), shape((cz.T, cz.CP), BF), shape((2, cz.rows, cz.CP), F32)),
        False, (moved.reshape(cz.T, cz.CP), cotangent.reshape(cz.T, channels)) + weights, "columns",
    )
    each = up(up(4 * rz.rows, slides) // slides, 2 * SUB)
    block = (each, rz.CP)
    grad_rows, total = call(
        functools.partial(rows_backward, slides, bands, each), rz,
        (shape((channels, width), BF), shape((slides,) + block, F32)),
        True, (v, t, grad_cols.reshape(moved_shape), grads_v) + weights, "rows_backward",
        [pltpu.VMEM(moved_shape, BF), dma((bands,)), dma((bands,)), pltpu.VMEM((2, rz.rows, rz.CP), F32)]
        + [
            pltpu.VMEM((slides,) + block, BF), pltpu.VMEM((slides,) + block, BF),
            pltpu.VMEM(block, BF), pltpu.VMEM((bands,) + block, BF),
            pltpu.VMEM(block, BF), pltpu.VMEM((slides,) + block, BF),
        ]
        + [dma((count,)) for count in (slides, slides, bands, bands, slides, slides)],
        1,
    )
    total = total.reshape(slides * each, rz.CP)[: 4 * rz.rows].reshape(4, rz.rows, rz.CP)
    at = rz.XR + rz.DR
    return (
        mixed.reshape(cotangent.shape),
        jnp.swapaxes(grad_rows, 0, 1).reshape(features.shape),
        jnp.swapaxes(total[:, : rank + 2 * states, :channels], 1, 2),
        total[:, rz.XR : rz.XR + rank, :channels],
        total[:, at, :channels],
        total[:, at + SUB : at + SUB + states, :channels],
        total[:, at + 1, :channels],
    )


def solution(mesh):
    in_specs = (
        P(("groups", "slide"), "band", None, None),
        P(("groups", "slide"), "band", None),
        P(("groups", "slide"), None, "band", None),
        P(), P(), P(), P(), P(),
    )
    out_specs = (
        P(("groups", "slide"), None, "band", None),
        P(("groups", "slide"), "band", None, None),
        P("groups", None, None),
        P("groups", None, None),
        P("groups", None),
        P("groups", None, None),
        P("groups", None),
    )
    return jax.shard_map(shards, mesh=mesh, in_specs=in_specs, out_specs=out_specs, check_vma=False)
```
